512 devices in a mesh: outer: 64 (over z_lo, y, core), inner: 8 (over z_hi, x).
Axes of the slice: x: 4, y: 8, z: 8 (z_hi: 2, z_lo: 4; z = z_hi * 4 + z_lo), core: 2. Of those that a mesh axis runs over, the one named last changes fastest.
Arguments:
- query_nope: bfloat16 [65536, 2048], P(('outer', 'inner')), may hold values from -400 to 400
- query_rope: bfloat16 [65536, 1024], P(('outer', 'inner')), may hold values from -6 to 6
- latent: bfloat16 [65536, 512], P(('outer', 'inner')), may hold values from -6 to 6
- key_rope: bfloat16 [65536, 64], P(('outer', 'inner')), may hold values from -6 to 6
- teacher_query: bfloat16 [65536, 2048], P(('outer', 'inner')), may hold values from -400 to 400
- teacher_key: bfloat16 [65536, 2048], P(('outer', 'inner')), may hold values from -6 to 6
- up_weight: bfloat16 [16, 128, 512], replicated, may hold values from -0.25 to 0.25
- kl_weight: float32 [65536, 16], P(('outer', 'inner')), may hold values from 30 to 300
- key_back: int32 [512], P(('outer', 'inner')), may hold values from 0 to 3, as said below
- valid_len: int32 [512], replicated, may hold values from 1 to 128, as said below
Outputs:
- d_query_nope: bfloat16 [65536, 2048], P(('outer', 'inner'))
- d_query_rope: bfloat16 [65536, 1024], P(('outer', 'inner'))
- d_latent: float32 [65536, 512], P(('outer', 'inner'))
- d_key_rope: float32 [65536, 64], P(('outer', 'inner'))
The draws below stay inside these ranges and needn't reach their ends.
Inputs may be any that keep to these rules, and one draw needn't show every extreme that they name: key_back[b] <= b, and some block has key_back equal to 3. `valid_len`: some block is full.
All inputs are finite; a program needn't handle non-finite values.
Results may differ from the reference program's by a relative error of at most 0.012.
The reference program's roundings to bfloat16 on the way (of `absorbed`, `grad_logit` and `d_absorbed`) count: a program that leaves them out, or rounds other values in their place, can miss the bound.
Values may be sent and summed in bfloat16 or wider, within the bound.
No kernel may reach another device: no remote copies, remote signals or barrier semaphores. Data moves between devices by JAX's collectives and lax.ppermute only.
A program may use at most 64 MiB of HBM per device.

```python
import math
import jax
import jax.numpy as jnp
from jax import lax

HEADS = 16
HEAD = 128
LATENT = 512
ROPE = 64
TEACHER_HEAD = 128
TOK_DEV = 128
SPAN = 4
BLOCKS = 512
TOKENS = 65536


def query_like(key, width):
    values = jnp.clip(jax.random.normal(key, (TOKENS, width), jnp.float32), -6.0, 6.0)
    return values


def key_like(key, width):
    values = jnp.clip(jax.random.normal(key, (TOKENS, width), jnp.float32), -6.0, 6.0)
    return values


def draw_query_nope(key, part):
    key = jax.random.fold_in(key, 1)
    return query_like(key, HEADS * HEAD).astype(jnp.bfloat16)


def draw_teacher_query(key, part):
    key = jax.random.fold_in(key, 2)
    return query_like(key, HEADS * TEACHER_HEAD).astype(jnp.bfloat16)


def draw_latent(key, part):
    own_key = jax.random.fold_in(key, 3)
    return key_like(own_key, LATENT).astype(jnp.bfloat16)


def draw_key_rope(key, part):
    own_key = jax.random.fold_in(key, 4)
    return key_like(own_key, ROPE).astype(jnp.bfloat16)


def draw_teacher_key(key, part):
    own_key = jax.random.fold_in(key, 5)
    return key_like(own_key, HEADS * TEACHER_HEAD).astype(jnp.bfloat16)


def draw_key_back(key, part):
    key = jax.random.fold_in(key, 6)
    index = jnp.arange(BLOCKS, dtype=jnp.int32)
    back = jnp.minimum(jax.random.randint(key, (BLOCKS,), 0, SPAN), index)
    forced = jax.random.randint(jax.random.fold_in(key, 1), (), SPAN - 1, BLOCKS)
    return jnp.where(index == forced, SPAN - 1, back).astype(jnp.int32)


def draw_valid_len(key, part):
    key = jax.random.fold_in(key, 7)
    index = jnp.arange(BLOCKS, dtype=jnp.int32)
    full = jax.random.randint(key, (BLOCKS,), 0, 2) == 1
    partial_len = jax.random.randint(jax.random.fold_in(key, 1), (BLOCKS,), TOK_DEV // 4, TOK_DEV + 1)
    forced = jax.random.randint(jax.random.fold_in(key, 2), (), 0, BLOCKS)
    lengths = jnp.where(full | (index == forced), TOK_DEV, partial_len)
    return lengths.astype(jnp.int32)


def levels(key, extent, pieces, least, high):
    def one(axis_at, parts):
        steps = jax.random.uniform(jax.random.fold_in(jax.random.fold_in(key, 6), axis_at), (parts,), jnp.float32, least / len(pieces), high / len(pieces))
        return jnp.repeat(jnp.exp(steps), extent[axis_at] // parts).reshape((-1,) + (1,) * (len(extent) - axis_at - 1))

    factor_of = one(*pieces[0])
    for cut in pieces[1:]:
        factor_of = factor_of * one(*cut)
    return factor_of


def centred(stream_key, dims, scale, reach, cuts=(), held_as=jnp.bfloat16):
    array = jax.random.normal(stream_key, dims, jnp.float32) * scale
    if len(cuts) > 0:
        array = levels(stream_key, dims, cuts, -0.22, 0.18) * array
    return jnp.clip(array, min=-reach, max=reach).astype(held_as)


def setup_inputs(seed: int = 0) -> dict:
    seeds = jax.random.split(jax.random.key(seed), 11)
    return {
        "query_nope": draw_query_nope(jax.random.fold_in(seeds[10], 71), 0),
        "query_rope": centred(seeds[1], (TOKENS, HEADS * ROPE), 1.0, 6.0, ((0, 512),)),
        "latent": draw_latent(jax.random.fold_in(seeds[10], 71), 0),
        "key_rope": draw_key_rope(jax.random.fold_in(seeds[10], 71), 0),
        "teacher_query": draw_teacher_query(jax.random.fold_in(seeds[10], 71), 0),
        "teacher_key": draw_teacher_key(jax.random.fold_in(seeds[10], 71), 0),
        "up_weight": centred(seeds[6], (HEADS, HEAD, LATENT), LATENT ** -0.5, 0.25),
        "kl_weight": jnp.clip(jnp.exp(math.log(300.0) - 2.3025851 * jax.random.uniform(seeds[7], (TOKENS, HEADS), jnp.float32) ** levels(seeds[7], (TOKENS, HEADS), ((0, 512),), -0.2, 0.2)), 30.0, 300.0),
        "key_back": draw_key_back(jax.random.fold_in(seeds[10], 71), 0),
        "valid_len": draw_valid_len(jax.random.fold_in(seeds[10], 71), 0),
    }


def slot_mask(reach_back, slot_lengths, own_length, tok_count, span_count):
    query_pos = jnp.arange(tok_count, dtype=jnp.int32)[:, None, None]
    key_pos = jnp.arange(tok_count, dtype=jnp.int32)[None, None, :]
    distance = (span_count - 1 - jnp.arange(span_count, dtype=jnp.int32))[None, :, None]
    allowed = (distance <= reach_back) & (key_pos < slot_lengths[None, :, None]) & ((distance > 0) | (key_pos <= query_pos))
    live = jnp.arange(tok_count, dtype=jnp.int32) < own_length
    return (allowed.reshape(tok_count, span_count * tok_count), live)

def masked_softmax(logits, allowed):
    masked = jnp.where(allowed, logits, -1e+30)
    highest = lax.optimization_barrier(jnp.max(masked, axis=-1, keepdims=True))
    powers = jnp.where(allowed, jnp.exp(masked - highest), 0.0)
    return powers / lax.optimization_barrier(jnp.sum(powers, axis=-1, keepdims=True))

def block_grads(nope_rows, rope_rows, latent_keys, rope_keys, teach_rows, teach_keys, weight_full, row_weight, allowed, live):
    tok_count = nope_rows.shape[0]
    key_count = latent_keys.shape[0]
    factor_student = 1.0 / math.sqrt(HEAD + ROPE)
    factor_teacher = 1.0 / math.sqrt(TEACHER_HEAD)
    nope_f = nope_rows.astype(jnp.float32).reshape(tok_count, HEADS, HEAD)
    rope_f = rope_rows.astype(jnp.float32).reshape(tok_count, HEADS, ROPE)
    teach_f = teach_rows.astype(jnp.float32).reshape(tok_count, HEADS, TEACHER_HEAD)
    tkeys_f = teach_keys.astype(jnp.float32).reshape(key_count, HEADS, TEACHER_HEAD)
    latent_f = latent_keys.astype(jnp.float32)
    rkeys_f = rope_keys.astype(jnp.float32)
    absorbed = jnp.einsum('thd,hdl->thl', nope_f, weight_full).astype(jnp.bfloat16)
    absorbed_f = absorbed.astype(jnp.float32)
    student = (jnp.einsum('thl,kl->htk', absorbed_f, latent_f) + jnp.einsum('thr,kr->htk', rope_f, rkeys_f)) * factor_student
    teacher = jnp.einsum('thd,khd->htk', teach_f, tkeys_f) * factor_teacher
    p_student = masked_softmax(student, allowed[None])
    p_teacher = masked_softmax(teacher, allowed[None])
    coeff = (row_weight.T * live.astype(jnp.float32)[None, :])[:, :, None]
    grad_logit = (coeff * (p_student - p_teacher)).astype(jnp.bfloat16)
    grad_f = grad_logit.astype(jnp.float32)
    d_absorbed = (jnp.einsum('htk,kl->thl', grad_f, latent_f) * factor_student).astype(jnp.bfloat16)
    d_nope = jnp.einsum('thl,hdl->thd', d_absorbed.astype(jnp.float32), weight_full).astype(jnp.bfloat16)
    d_rope_q = (jnp.einsum('htk,kr->thr', grad_f, rkeys_f) * factor_student).astype(jnp.bfloat16)
    d_latent = jnp.einsum('htk,thl->kl', grad_f, absorbed_f) * factor_student
    d_rope_k = jnp.einsum('htk,thr->kr', grad_f, rope_f) * factor_student
    return (d_nope.reshape(tok_count, HEADS * HEAD), d_rope_q.reshape(tok_count, HEADS * ROPE), d_latent, d_rope_k)

def reference(query_nope, query_rope, latent, key_rope, teacher_query, teacher_key, up_weight, kl_weight, key_back, valid_len):
    front = (SPAN - 1) * TOK_DEV

    def padded(values):
        return jnp.concatenate([jnp.zeros((front, values.shape[1]), values.dtype), values], axis=0)
    latent_pad = padded(latent)
    rope_pad = padded(key_rope)
    teach_pad = padded(teacher_key)
    lengths_pad = jnp.concatenate([jnp.ones((SPAN - 1,), jnp.int32), valid_len.astype(jnp.int32)])
    weight_full = up_weight.astype(jnp.float32)
    width = LATENT + ROPE

    def step(gradients, block):
        start = (block * TOK_DEV).astype(jnp.int32)
        nope_rows = lax.dynamic_slice_in_dim(query_nope, start, TOK_DEV, 0)
        rope_rows = lax.dynamic_slice_in_dim(query_rope, start, TOK_DEV, 0)
        teach_rows = lax.dynamic_slice_in_dim(teacher_query, start, TOK_DEV, 0)
        row_weight = lax.dynamic_slice_in_dim(kl_weight, start, TOK_DEV, 0)
        latent_keys = lax.dynamic_slice_in_dim(latent_pad, start, SPAN * TOK_DEV, 0)
        rope_keys = lax.dynamic_slice_in_dim(rope_pad, start, SPAN * TOK_DEV, 0)
        teach_keys = lax.dynamic_slice_in_dim(teach_pad, start, SPAN * TOK_DEV, 0)
        slot_lengths = lax.dynamic_slice_in_dim(lengths_pad, block.astype(jnp.int32), SPAN, 0)
        reach_back = lax.dynamic_slice_in_dim(key_back.astype(jnp.int32), block.astype(jnp.int32), 1, 0)[0]
        allowed, live = slot_mask(reach_back, slot_lengths, slot_lengths[SPAN - 1], TOK_DEV, SPAN)
        d_nope, d_rope_q, d_latent, d_rope_k = block_grads(nope_rows, rope_rows, latent_keys, rope_keys, teach_rows, teach_keys, weight_full, row_weight, allowed, live)
        partial_grad = jnp.concatenate([d_latent, d_rope_k], axis=1)
        updated = lax.dynamic_slice_in_dim(gradients, start, SPAN * TOK_DEV, 0) + partial_grad
        gradients = lax.dynamic_update_slice_in_dim(gradients, updated, start, 0)
        return (gradients, (d_nope, d_rope_q))
    initial = jnp.zeros((front + TOKENS, width), jnp.float32)
    gradients, outputs = lax.scan(step, initial, jnp.arange(BLOCKS, dtype=jnp.int32))
    d_query_nope = outputs[0].reshape(TOKENS, HEADS * HEAD)
    d_query_rope = outputs[1].reshape(TOKENS, HEADS * ROPE)
    d_latent = gradients[front:, :LATENT]
    d_key_rope = gradients[front:, LATENT:]
    return (d_query_nope, d_query_rope, d_latent, d_key_rope)
```

```python
import functools
import math

import jax
import jax.numpy as jnp
from jax import lax
from jax.experimental import pallas as pl
from jax.experimental.pallas import tpu as pltpu
from jax.sharding import PartitionSpec as P

HEADS = 16
HEAD = 128
LATENT = 512
ROPE = 64
TOK = 128
SPAN = 4
KEYS = SPAN * TOK
WIDE = LATENT + 2 * ROPE
PAIRS = HEADS // 2
FIRST = 3
RING = 4
AXES = ("outer", "inner")
F_STUDENT = 1.0 / math.sqrt(HEAD + ROPE)
F_TEACHER = 1.0 / math.sqrt(HEAD)
LOG2E = math.log2(math.e)
VMEM_LIMIT = 48 * 1024 * 1024

NN = (((1,), (0,)), ((), ()))
NT = (((1,), (1,)), ((), ()))


def dot(a, b, dims=NN):
    return lax.dot_general(a, b, dims, preferred_element_type=jnp.float32)


def along_x(step, sources):
    def route(count):
        return [
            (b, b - b % RING + (b + step) % RING) for b in range(count) if b % RING in sources
        ]

    return route


def next_run(count):
    return [(b, b + RING) for b in range(count - RING)]


def permute(value, route):
    return lax.ppermute(value, AXES, route(lax.axis_size(AXES)))


def softmax_parts(logits):
    powers = jnp.exp2(logits - jnp.max(logits, axis=0, keepdims=True))
    return powers, jnp.sum(powers, axis=0, keepdims=True)


def from_slots(place, sources, act):
    own, own1, own2, rotated, crossed, back, around = sources
    act(0, own)
    for distance, here, earlier, first in ((1, own1, around, 1), (2, own2, back, 2), (3, rotated, crossed, 3)):
        pl.when(place >= first)(functools.partial(act, distance, here))
        pl.when(place < first)(functools.partial(act, distance, earlier))


def student_kernel(
    scalar_ref, length_ref, nope_ref, rope_ref, up_ref, kl_ref, *refs
):
    sources, (mixed_ref, p_ref, bias_ref, coeff_ref, lr_ref, lrt_ref, sems) = refs[:7], refs[7:]
    step = pl.program_id(0)
    position = scalar_ref[0]
    starts = [HEADS * HEAD] * 3 + [FIRST * 2 * HEAD] * 4
    place = position % RING

    @pl.when(step == 0)
    def _():
        columns = dict(zip(map(id, sources), starts))

        def copy(distance, source):
            return pltpu.make_async_copy(
                source.at[:, pl.ds(columns[id(source)], WIDE)],
                lr_ref.at[pl.ds(distance * TOK, TOK)],
                sems.at[distance],
            )

        from_slots(place, sources, lambda distance, source: copy(distance, source).start())
        query = lax.broadcasted_iota(jnp.int32, (TOK, TOK), 1)
        key = lax.broadcasted_iota(jnp.int32, (TOK, TOK), 0)
        for distance in range(SPAN):
            length = length_ref[jnp.maximum(position - distance, 0)]
            length = jnp.where(distance <= scalar_ref[1], length, 0)
            allowed = key < length
            if distance == 0:
                allowed = allowed & (key <= query)
            bias_ref[pl.ds(distance * TOK, TOK), :] = jnp.where(allowed, 0.0, -1e30)
        live = lax.broadcasted_iota(jnp.int32, (HEADS, TOK), 1) < length_ref[position]
        coeff_ref[...] = jnp.where(live, kl_ref[...].T, 0.0)
        for distance in range(SPAN):
            copy(distance, sources[0] if distance < 3 else sources[3]).wait()
        lrt_ref[...] = lr_ref[...].T

    lane = lax.broadcasted_iota(jnp.int32, (TOK, 2 * ROPE), 1)
    rope = rope_ref[...]
    for half in range(2):
        rows = pl.ds(half * TOK, TOK)
        absorbed = dot(nope_ref[:, pl.ds(half * HEAD, HEAD)], up_ref[half])
        mixed_ref[rows, pl.ds(0, LATENT)] = absorbed.astype(jnp.bfloat16)
        kept = (lane < ROPE) if half == 0 else (lane >= ROPE)
        mixed_ref[rows, pl.ds(LATENT, 2 * ROPE)] = jnp.where(kept, rope, jnp.zeros_like(rope))
    logits = dot(lr_ref[...], mixed_ref[...], NT)
    for half in range(2):
        columns = slice(half * TOK, (half + 1) * TOK)
        powers, total = softmax_parts(logits[:, columns] * (F_STUDENT * LOG2E) + bias_ref[...])
        weight = coeff_ref[pl.ds(2 * step + half, 1), :]
        p_ref[:, columns] = powers * (weight / total)


def teacher_kernel(first, pairs, last, scalar_ref, *refs):
    sources, refs = refs[:7], refs[7:]
    (query_ref, p_ref, bias_ref, coeff_ref, mixed_ref), refs = refs[:5], refs[5:]
    if last:
        sum_ref, g_ref, own_ref, *sent_refs = refs[:6]
    else:
        g_ref, sum_out_ref = refs[:2]
    acc_ref, keys_ref, diagonal_ref, sems = refs[-4:]
    step = pl.program_id(0)
    place = scalar_ref[0] % RING
    starts = [first * 2 * HEAD] * 3 + [0] * 4
    columns = dict(zip(map(id, sources), starts))

    def copy(pair, distance, source):
        return pltpu.make_async_copy(
            source.at[:, pl.ds(columns[id(source)] + pair * 2 * HEAD, 2 * HEAD)],
            keys_ref.at[pair, pl.ds(distance * TOK, TOK)],
            sems.at[pair, distance],
        )

    @pl.when(step == 0)
    def _():
        for pair in range(pairs):
            from_slots(
                place, sources, lambda distance, source, pair=pair: copy(pair, distance, source).start()
            )
        diagonal_ref[...] = jnp.zeros_like(diagonal_ref)
        if last:
            acc_ref[...] = sum_ref[...]
        else:
            acc_ref[...] = jnp.zeros_like(acc_ref)

    for half in range(2):
        block = pl.ds(half * HEAD, HEAD)
        diagonal_ref[block, block] = query_ref[:, block]
    for pair in range(pairs):

        @pl.when(step == pair)
        def _(pair=pair):
            for distance in range(SPAN):
                copy(pair, distance, sources[0] if distance < 3 else sources[3]).wait()

    logits = dot(keys_ref[step], diagonal_ref[...], NT)
    for half in range(2):
        cols = slice(half * TOK, (half + 1) * TOK)
        powers, total = softmax_parts(logits[:, cols] * (F_TEACHER * LOG2E) + bias_ref[...])
        weight = coeff_ref[pl.ds(2 * (first + step) + half, 1), :]
        g_ref[:, cols] = (p_ref[:, cols] - powers * (weight / total)).astype(jnp.bfloat16)
    acc_ref[...] += dot(g_ref[...], mixed_ref[...])

    @pl.when(step == pairs - 1)
    def _():
        if last:
            own_ref[...] = acc_ref[pl.ds(0, TOK), :] * F_STUDENT
            for distance in range(1, SPAN):
                sent_refs[distance - 1][...] = (
                    acc_ref[pl.ds(distance * TOK, TOK), :] * F_STUDENT
                ).astype(jnp.bfloat16)
        else:
            sum_out_ref[...] = acc_ref[...]


def query_kernel(g_ref, lrt_ref, up_ref, nope_out_ref, rope_out_ref):
    grads = (dot(lrt_ref[...], g_ref[...]) * F_STUDENT).astype(jnp.bfloat16)
    ropes = []
    for half in range(2):
        block = slice(half * TOK, (half + 1) * TOK)
        turned = dot(up_ref[half], grads[:LATENT, block])
        nope_out_ref[:, block] = turned.T.astype(jnp.bfloat16)
        ropes.append(grads[LATENT + half * ROPE : LATENT + (half + 1) * ROPE, block])
    rope_out_ref[...] = jnp.concatenate(ropes, axis=0).astype(jnp.float32).T.astype(jnp.bfloat16)


def shape(*dims, dtype=jnp.bfloat16):
    return jax.ShapeDtypeStruct(dims, dtype)


SMEM = pl.BlockSpec(memory_space=pltpu.SMEM)
ANY = pl.BlockSpec(memory_space=pl.ANY)


def whole(*dims):
    return pl.BlockSpec(dims, lambda i: (0,) * len(dims))


def params():
    return pltpu.CompilerParams(
        dimension_semantics=("arbitrary",), vmem_limit_bytes=VMEM_LIMIT
    )


def student_call(scalars, valid_len, nope, rope, up_weight, kl_weight, sources):
    return pl.pallas_call(
        student_kernel,
        grid=(PAIRS,),
        in_specs=[
            SMEM,
            SMEM,
            pl.BlockSpec((TOK, 2 * HEAD), lambda i: (0, i)),
            pl.BlockSpec((TOK, 2 * ROPE), lambda i: (0, i)),
            pl.BlockSpec((2, HEAD, LATENT), lambda i: (i, 0, 0)),
            whole(TOK, HEADS),
        ]
        + [ANY] * 7,
        out_specs=[
            pl.BlockSpec((2 * TOK, WIDE), lambda i: (i, 0)),
            pl.BlockSpec((KEYS, 2 * TOK), lambda i: (0, i)),
            whole(KEYS, TOK),
            whole(HEADS, TOK),
            whole(KEYS, WIDE),
            whole(WIDE, KEYS),
        ],
        out_shape=[
            shape(HEADS * TOK, WIDE),
            shape(KEYS, HEADS * TOK, dtype=jnp.float32),
            shape(KEYS, TOK, dtype=jnp.float32),
            shape(HEADS, TOK, dtype=jnp.float32),
            shape(KEYS, WIDE),
            shape(WIDE, KEYS),
        ],
        scratch_shapes=[pltpu.SemaphoreType.DMA((SPAN,))],
        compiler_params=params(),
        cost_estimate=pl.CostEstimate(
            flops=2 * HEADS * TOK * (HEAD * LATENT + KEYS * WIDE),
            bytes_accessed=12_000_000,
            transcendentals=HEADS * TOK * KEYS,
        ),
    )(scalars, valid_len, nope, rope, up_weight, kl_weight, *sources)


def teacher_call(first, pairs, last, scalars, sources, teacher_query, p, bias, coeff, mixed, summed=None):
    outs = [(pl.BlockSpec((KEYS, 2 * TOK), lambda i: (0, i)), shape(KEYS, pairs * 2 * TOK))]
    if last:
        outs.append((whole(TOK, WIDE), shape(TOK, WIDE, dtype=jnp.float32)))
        outs += [(whole(TOK, WIDE), shape(TOK, WIDE))] * 3
    else:
        outs.append((whole(KEYS, WIDE), shape(KEYS, WIDE, dtype=jnp.float32)))
    return pl.pallas_call(
        functools.partial(teacher_kernel, first, pairs, last),
        grid=(pairs,),
        in_specs=[SMEM]
        + [ANY] * 7
        + [
            pl.BlockSpec((TOK, 2 * HEAD), lambda i: (0, first + i)),
            pl.BlockSpec((KEYS, 2 * TOK), lambda i: (0, first + i)),
            whole(KEYS, TOK),
            whole(HEADS, TOK),
            pl.BlockSpec((2 * TOK, WIDE), lambda i: (first + i, 0)),
        ]
        + ([whole(KEYS, WIDE)] if last else []),
        out_specs=[spec for spec, _ in outs],
        out_shape=[form for _, form in outs],
        scratch_shapes=[
            pltpu.VMEM((KEYS, WIDE), jnp.float32),
            pltpu.VMEM((pairs, KEYS, 2 * HEAD), jnp.bfloat16),
            pltpu.VMEM((2 * TOK, 2 * HEAD), jnp.bfloat16),
            pltpu.SemaphoreType.DMA((pairs, SPAN)),
        ],
        compiler_params=params(),
        cost_estimate=pl.CostEstimate(
            flops=4 * pairs * TOK * KEYS * (2 * HEAD + WIDE),
            bytes_accessed=pairs * 1_500_000,
            transcendentals=2 * pairs * TOK * KEYS,
        ),
    )(scalars, *sources, teacher_query, p, bias, coeff, mixed, *([summed] if last else []))


def query_call(first, pairs, g, lrt, up_weight):
    return pl.pallas_call(
        query_kernel,
        grid=(pairs,),
        in_specs=[
            pl.BlockSpec((KEYS, 2 * TOK), lambda i: (0, i)),
            whole(WIDE, KEYS),
            pl.BlockSpec((2, HEAD, LATENT), lambda i: (first + i, 0, 0)),
        ],
        out_specs=[
            pl.BlockSpec((TOK, 2 * HEAD), lambda i: (0, i)),
            pl.BlockSpec((TOK, 2 * ROPE), lambda i: (0, i)),
        ],
        out_shape=[shape(TOK, pairs * 2 * HEAD), shape(TOK, pairs * 2 * ROPE)],
        compiler_params=params(),
        cost_estimate=pl.CostEstimate(
            flops=4 * pairs * TOK * LATENT * (WIDE + HEAD),
            bytes_accessed=pairs * 800_000,
            transcendentals=0,
        ),
    )(g, lrt, up_weight)


def on_device(
    query_nope,
    query_rope,
    latent,
    key_rope,
    teacher_query,
    teacher_key,
    up_weight,
    kl_weight,
    key_back,
    valid_len,
):
    position = lax.axis_index(AXES)
    place = position % RING
    scalars = jnp.stack([position.astype(jnp.int32), key_back[0]])

    cut = FIRST * 2 * HEAD
    rows = jnp.concatenate([latent, key_rope, key_rope], axis=1)
    own = jnp.concatenate([teacher_key, rows], axis=1)
    parts = (jnp.concatenate([teacher_key[:, :cut], rows], axis=1), teacher_key[:, cut:])

    rotated = [permute(part, along_x(-1, (0, 1, 2, 3))) for part in parts]
    own1 = permute(own, along_x(1, (0, 1, 2)))
    own2 = permute(own, along_x(2, (0, 1)))
    chunks = []
    earlier = None
    for part, turned in zip(parts, rotated):
        leaving = jnp.where(place == RING - 1, part, turned)
        if earlier is not None:
            leaving = lax.optimization_barrier((leaving, earlier))[0]
        crossed = permute(leaving, next_run)
        back = permute(crossed, along_x(-1, (1, 2)))
        around = permute(crossed, along_x(1, (3,)))
        chunks.append((own, own1, own2, turned, crossed, back, around))
        earlier = crossed

    mixed, p, bias, coeff, _, lrt = student_call(
        scalars, valid_len, query_nope, query_rope, up_weight, kl_weight, chunks[0]
    )
    g0, summed = teacher_call(
        0, FIRST, False, scalars, chunks[0], teacher_query, p, bias, coeff, mixed
    )
    g1, kept, *sent = teacher_call(
        FIRST, PAIRS - FIRST, True, scalars, chunks[1], teacher_query, p, bias, coeff, mixed, summed
    )
    nope0, rope0 = query_call(0, FIRST, g0, lrt, up_weight)
    nope1, rope1 = query_call(FIRST, PAIRS - FIRST, g1, lrt, up_weight)

    total = kept
    for distance in range(1, SPAN):
        total = total + lax.ppermute(
            sent[distance - 1],
            AXES,
            [(b, b - distance) for b in range(distance, lax.axis_size(AXES))],
        ).astype(jnp.float32)
    d_latent = total[:, :LATENT]
    d_key_rope = total[:, LATENT : LATENT + ROPE] + total[:, LATENT + ROPE :]
    return (
        jnp.concatenate([nope0, nope1], axis=1),
        jnp.concatenate([rope0, rope1], axis=1),
        d_latent,
        d_key_rope,
    )


def solution(mesh):
    split = P(AXES, None)
    return jax.shard_map(
        on_device,
        mesh=mesh,
        in_specs=(split,) * 6 + (P(), split, P(AXES), P()),
        out_specs=(split,) * 4,
        check_vma=False,
    )
```

```python
import functools
import math

import jax
import jax.numpy as jnp
from jax import lax
from jax.experimental import pallas as pl
from jax.experimental.pallas import tpu as pltpu
from jax.sharding import PartitionSpec as P

HEADS = 16
HEAD = 128
LATENT = 512
ROPE = 64
TOK = 128
SPAN = 4
KEYS = SPAN * TOK
WIDE = LATENT + 2 * ROPE
PAIRS = HEADS // 2
FIRST = 3
CUT = FIRST * 2 * HEAD
REST = HEADS * HEAD - CUT
RING = 4
AXES = ("outer", "inner")
F_STUDENT = 1.0 / math.sqrt(HEAD + ROPE)
F_TEACHER = 1.0 / math.sqrt(HEAD)
LOG2E = math.log2(math.e)
VMEM_LIMIT = 20 * 1024 * 1024

NN = (((1,), (0,)), ((), ()))
NT = (((1,), (1,)), ((), ()))


def dot(a, b, dims=NN):
    return lax.dot_general(a, b, dims, preferred_element_type=jnp.float32)


def along_x(step, sources):
    def route(count):
        return [
            (b, b - b % RING + (b + step) % RING) for b in range(count) if b % RING in sources
        ]

    return route


def next_run(count):
    return [(b, b + RING) for b in range(count - RING)]


def permute(value, route):
    return lax.ppermute(value, AXES, route(lax.axis_size(AXES)))


def softmax_parts(logits):
    powers = jnp.exp2(logits - jnp.max(logits, axis=0, keepdims=True))
    return powers, jnp.sum(powers, axis=0, keepdims=True)


def from_slots(place, sources, act):
    if len(sources) == SPAN:
        for distance in range(SPAN):
            act(distance, sources[distance])
        return
    own, own1, own2, rotated, crossed, back, around = sources
    act(0, own)
    for distance, here, earlier in ((1, own1, around), (2, own2, back), (3, rotated, crossed)):
        pl.when(place >= distance)(functools.partial(act, distance, here))
        pl.when(place < distance)(functools.partial(act, distance, earlier))


def pack_kernel(latent_ref, rope_ref, key_ref, first_ref, rest_ref, sems):
    copies = [
        pltpu.make_async_copy(key_ref.at[:, pl.ds(0, CUT)], first_ref.at[:, pl.ds(0, CUT)], sems.at[0]),
        pltpu.make_async_copy(latent_ref, first_ref.at[:, pl.ds(CUT, LATENT)], sems.at[1]),
        pltpu.make_async_copy(key_ref.at[:, pl.ds(CUT, REST)], rest_ref, sems.at[2]),
    ]
    for copy in copies:
        copy.start()
    rope = rope_ref[...].astype(jnp.float32)
    both = jnp.concatenate([rope, rope], axis=0).T.astype(jnp.bfloat16)
    first_ref[:, CUT + LATENT :] = both
    for copy in copies:
        copy.wait()


def absorb_kernel(nope_ref, rope_ref, up_ref, mixed_ref):
    lane = lax.broadcasted_iota(jnp.int32, (TOK, 2 * ROPE), 1)
    for head in range(HEADS):
        rows = slice(head * TOK, (head + 1) * TOK)
        absorbed = dot(nope_ref[:, head * HEAD : (head + 1) * HEAD], up_ref[head])
        mixed_ref[rows, :LATENT] = absorbed.astype(jnp.bfloat16)
        rope = rope_ref[:, (head // 2) * 2 * ROPE : (head // 2 + 1) * 2 * ROPE]
        kept = (lane < ROPE) if head % 2 == 0 else (lane >= ROPE)
        mixed_ref[rows, LATENT:] = jnp.where(kept, rope, jnp.zeros_like(rope))


def student_kernel(scalar_ref, length_ref, kl_ref, mixed_ref, *refs):
    sources, (p_ref, bias_ref, coeff_ref, lrt_ref, lr_ref, sems) = refs[:SPAN], refs[SPAN:]
    position = scalar_ref[0]
    place = position % RING

    def copy(distance, source):
        return pltpu.make_async_copy(
            source.at[:, pl.ds(CUT, WIDE)],
            lr_ref.at[pl.ds(distance * TOK, TOK)],
            sems.at[distance],
        )

    from_slots(place, sources, lambda distance, source: copy(distance, source).start())
    query = lax.broadcasted_iota(jnp.int32, (TOK, TOK), 1)
    key = lax.broadcasted_iota(jnp.int32, (TOK, TOK), 0)
    for distance in range(SPAN):
        length = length_ref[jnp.maximum(position - distance, 0)]
        length = jnp.where(distance <= scalar_ref[1], length, 0)
        allowed = key < length
        if distance == 0:
            allowed = allowed & (key <= query)
        bias_ref[distance * TOK : (distance + 1) * TOK, :] = jnp.where(allowed, 0.0, -1e30)
    live = lax.broadcasted_iota(jnp.int32, (HEADS, TOK), 1) < length_ref[position]
    coeff_ref[...] = jnp.where(live, kl_ref[...], 0.0)
    for distance in range(SPAN):
        copy(distance, sources[distance]).wait()
    for pair in range(PAIRS):
        logits = dot(lr_ref[...], mixed_ref[pair * 2 * TOK : (pair + 1) * 2 * TOK, :], NT)
        for half in range(2):
            head = 2 * pair + half
            powers, total = softmax_parts(
                logits[:, half * TOK : (half + 1) * TOK] * (F_STUDENT * LOG2E) + bias_ref[...]
            )
            weight = coeff_ref[head : head + 1, :]
            p_ref[:, head * TOK : (head + 1) * TOK] = powers * (weight / total)
    lrt_ref[...] = lr_ref[...].T


def teacher_kernel(first, pairs, start, scalar_ref, *refs):
    count = len(start)
    last = first > 0
    sources, refs = refs[:count], refs[count:]
    (query_ref, p_ref, bias_ref, coeff_ref, mixed_ref), refs = refs[:5], refs[5:]
    if last:
        sum_ref, g_ref, own_ref, *sent_refs = refs[:6]
    else:
        g_ref, sum_out_ref = refs[:2]
    keys_ref, diagonal_ref, sems = refs[-3:]
    place = scalar_ref[0] % RING
    columns = dict(zip(map(id, sources), start))

    def copy(pair, distance, source):
        return pltpu.make_async_copy(
            source.at[:, pl.ds(columns[id(source)] + pair * 2 * HEAD, 2 * HEAD)],
            keys_ref.at[pair, pl.ds(distance * TOK, TOK)],
            sems.at[pair, distance],
        )

    for pair in range(pairs):
        from_slots(
            place, sources, lambda distance, source, pair=pair: copy(pair, distance, source).start()
        )
    diagonal_ref[...] = jnp.zeros_like(diagonal_ref)
    for pair in range(pairs):
        for half in range(2):
            block = slice(half * HEAD, (half + 1) * HEAD)
            head = 2 * pair + half
            diagonal_ref[pair, block, block] = query_ref[:, (2 * first + head) * HEAD : (2 * first + head + 1) * HEAD]
    for pair in range(pairs):
        for distance in range(SPAN):
            copy(pair, distance, sources[distance]).wait()
    for pair in range(pairs):
        logits = dot(keys_ref[pair], diagonal_ref[pair], NT)
        for half in range(2):
            head = 2 * pair + half
            powers, total = softmax_parts(
                logits[:, half * TOK : (half + 1) * TOK] * (F_TEACHER * LOG2E) + bias_ref[...]
            )
            full = 2 * first + head
            weight = coeff_ref[full : full + 1, :]
            student = p_ref[:, full * TOK : (full + 1) * TOK]
            g_ref[:, head * TOK : (head + 1) * TOK] = (student - powers * (weight / total)).astype(jnp.bfloat16)
    summed = dot(g_ref[...], mixed_ref[2 * first * TOK : 2 * (first + pairs) * TOK, :])
    if last:
        summed = (summed + sum_ref[...]) * F_STUDENT
        own_ref[...] = summed[:TOK]
        for distance in range(1, SPAN):
            sent_refs[distance - 1][...] = summed[distance * TOK : (distance + 1) * TOK].astype(
                jnp.bfloat16
            )
    else:
        sum_out_ref[...] = summed


def query_kernel(counts, *refs):
    g_refs, (lrt_ref, up_ref, nope_out_ref, rope_out_ref) = refs[: len(counts)], refs[len(counts) :]
    head = 0
    for g_ref, pairs in zip(g_refs, counts):
        for pair in range(pairs):
            grads = dot(lrt_ref[...], g_ref[:, pair * 2 * TOK : (pair + 1) * 2 * TOK]) * F_STUDENT
            grads = grads.astype(jnp.bfloat16)
            ropes = []
            for half in range(2):
                block = slice(half * TOK, (half + 1) * TOK)
                turned = dot(up_ref[head + half], grads[:LATENT, block])
                nope_out_ref[:, (head + half) * HEAD : (head + half + 1) * HEAD] = turned.T.astype(
                    jnp.bfloat16
                )
                ropes.append(grads[LATENT + half * ROPE : LATENT + (half + 1) * ROPE, block])
            both = jnp.concatenate(ropes, axis=0).astype(jnp.float32).T.astype(jnp.bfloat16)
            rope_out_ref[:, head * ROPE : (head + 2) * ROPE] = both
            head += 2


def shape(*dims, dtype=jnp.bfloat16):
    return jax.ShapeDtypeStruct(dims, dtype)


SMEM = pl.BlockSpec(memory_space=pltpu.SMEM)
ANY = pl.BlockSpec(memory_space=pl.ANY)
VMEM = pl.BlockSpec(memory_space=pltpu.VMEM)


def call(kernel, ins, outs, scratch, flops, accessed, exps=0, kept=True):
    return pl.pallas_call(
        kernel,
        in_specs=ins,
        out_specs=[VMEM] * len(outs),
        out_shape=[pltpu.VMEM(form.shape, form.dtype) for form in outs] if kept else outs,
        scratch_shapes=scratch,
        compiler_params=pltpu.CompilerParams(vmem_limit_bytes=VMEM_LIMIT),
        cost_estimate=pl.CostEstimate(flops=flops, bytes_accessed=accessed, transcendentals=exps),
    )


def finish_kernel(kept_ref, one_ref, two_ref, three_ref, latent_ref, rope_ref):
    total = kept_ref[...]
    for ref in (one_ref, two_ref, three_ref):
        total = total + ref[...].astype(jnp.float32)
    latent_ref[...] = total[:, :LATENT]
    turned = total[:, LATENT:].T
    rope_ref[...] = turned[:ROPE] + turned[ROPE:]


def pack_call(latent, key_rope, teacher_key):
    return call(
        pack_kernel,
        [ANY, VMEM, ANY],
        [shape(TOK, CUT + WIDE), shape(TOK, REST)],
        [pltpu.SemaphoreType.DMA((3,))],
        0,
        2_000_000,
    )(latent, key_rope.T, teacher_key)


def absorb_call(nope, rope, up_weight):
    return call(
        absorb_kernel,
        [VMEM] * 3,
        [shape(HEADS * TOK, WIDE)],
        [],
        2 * HEADS * TOK * HEAD * LATENT,
        6_000_000,
    )(nope, rope, up_weight)[0]


def student_call(scalars, valid_len, kl_weight, mixed, sources):
    return call(
        student_kernel,
        [SMEM, SMEM, VMEM, VMEM] + [ANY] * SPAN,
        [
            shape(KEYS, HEADS * TOK, dtype=jnp.float32),
            shape(KEYS, TOK, dtype=jnp.float32),
            shape(HEADS, TOK, dtype=jnp.float32),
            shape(WIDE, KEYS),
        ],
        [pltpu.VMEM((KEYS, WIDE), jnp.bfloat16), pltpu.SemaphoreType.DMA((SPAN,))],
        2 * HEADS * TOK * KEYS * WIDE,
        8_000_000,
        HEADS * TOK * KEYS,
    )(scalars, valid_len, kl_weight.T, mixed, *sources)


def teacher_call(first, pairs, start, scalars, sources, *operands):
    outs = [shape(KEYS, pairs * 2 * TOK)]
    if first > 0:
        outs += [shape(TOK, WIDE, dtype=jnp.float32)] + [shape(TOK, WIDE)] * 3
    else:
        outs += [shape(KEYS, WIDE, dtype=jnp.float32)]
    return call(
        functools.partial(teacher_kernel, first, pairs, start),
        [SMEM] + [ANY] * len(sources) + [VMEM] * len(operands),
        outs,
        [
            pltpu.VMEM((pairs, KEYS, 2 * HEAD), jnp.bfloat16),
            pltpu.VMEM((pairs, 2 * TOK, 2 * HEAD), jnp.bfloat16),
            pltpu.SemaphoreType.DMA((pairs, SPAN)),
        ],
        4 * pairs * TOK * KEYS * (2 * HEAD + WIDE),
        pairs * 1_500_000,
        2 * pairs * TOK * KEYS,
    )(scalars, *sources, *operands)


def query_call(counts, gs, lrt, up_weight):
    return call(
        functools.partial(query_kernel, counts),
        [VMEM] * (len(counts) + 2),
        [shape(TOK, HEADS * HEAD), shape(TOK, HEADS * ROPE)],
        [],
        4 * HEADS * TOK * LATENT * (KEYS + HEAD),
        6_000_000,
        kept=False,
    )(*gs, lrt, up_weight)


def finish_call(kept, received):
    return call(
        finish_kernel,
        [VMEM] * 4,
        [shape(TOK, LATENT, dtype=jnp.float32), shape(ROPE, TOK, dtype=jnp.float32)],
        [],
        0,
        1_000_000,
        kept=False,
    )(kept, *received)


def after(value, *others):
    return lax.optimization_barrier((value,) + others)[0]


def on_device(
    query_nope,
    query_rope,
    latent,
    key_rope,
    teacher_query,
    teacher_key,
    up_weight,
    kl_weight,
    key_back,
    valid_len,
):
    position = lax.axis_index(AXES)
    place = position % RING
    scalars = jnp.stack([position.astype(jnp.int32), key_back[0]])
    first, rest = pack_call(latent, key_rope, teacher_key)

    rotated = permute(rest, along_x(-1, (0, 1, 2, 3)))
    crossed_first = permute(first, next_run)
    crossed = permute(jnp.where(place == RING - 1, rest, rotated), next_run)
    later = after(rest, rotated)
    own1 = permute(later, along_x(1, (0, 1, 2)))
    own2 = permute(later, along_x(2, (0, 1)))
    everywhere = (0, 1, 2, 3)
    spread = [
        permute(jnp.where(place + step >= RING, crossed_first, first), along_x(step, everywhere))
        for step in (1, 2, 3)
    ]
    mixed = absorb_call(query_nope, query_rope, up_weight)
    chunk = (first, *spread)
    p, bias, coeff, lrt = student_call(scalars, valid_len, kl_weight, mixed, chunk)
    crossed = after(crossed, bias)
    back = permute(crossed, along_x(-1, (1, 2)))
    around = permute(crossed, along_x(1, (3,)))

    shared = (teacher_query, p, bias, coeff, mixed)
    g0, summed = teacher_call(0, FIRST, [0] * SPAN, scalars, chunk, *shared)
    chunk = (rest, own1, own2, rotated, crossed, back, around)
    g1, kept, *sent = teacher_call(FIRST, PAIRS - FIRST, [0] * 7, scalars, chunk, *shared, summed)

    received = [
        lax.ppermute(
            sent[distance - 1],
            AXES,
            [(b, b - distance) for b in range(distance, lax.axis_size(AXES))],
        )
        for distance in range(1, SPAN)
    ]
    d_nope, d_rope = query_call((FIRST, PAIRS - FIRST), (g0, g1), lrt, up_weight)
    d_latent, d_key_rope = finish_call(kept, received)
    return d_nope, d_rope, d_latent, d_key_rope.T


def solution(mesh):
    split = P(AXES, None)
    return jax.shard_map(
        on_device,
        mesh=mesh,
        in_specs=(split,) * 6 + (P(), split, P(AXES), P()),
        out_specs=(split,) * 4,
        check_vma=False,
    )
```

```python
import functools
import math

import jax
import jax.numpy as jnp
from jax import lax
from jax.experimental import pallas as pl
from jax.experimental.pallas import tpu as pltpu
from jax.sharding import PartitionSpec as P

HEADS = 16
HEAD = 128
LATENT = 512
ROPE = 64
TOK = 128
SPAN = 4
KEYS = SPAN * TOK
WIDE = LATENT + 2 * ROPE
PAIRS = HEADS // 2
FIRST = 3
CUT = FIRST * 2 * HEAD
REST = HEADS * HEAD - CUT
RING = 4
AXES = ("outer", "inner")
F_STUDENT = 1.0 / math.sqrt(HEAD + ROPE)
F_TEACHER = 1.0 / math.sqrt(HEAD)
LOG2E = math.log2(math.e)
VMEM_LIMIT = 20 * 1024 * 1024

NN = (((1,), (0,)), ((), ()))
NT = (((1,), (1,)), ((), ()))


def dot(a, b, dims=NN):
    return lax.dot_general(a, b, dims, preferred_element_type=jnp.float32)


def along_x(step, sources, leaves=None):
    def route(count):
        pairs = []
        for b in range(count):
            if b % RING in sources:
                to = b - b % RING + (b + step) % RING
                if leaves is not None and b % RING in leaves and b % (2 * RING) < RING:
                    to += 2 * RING
                if to < count:
                    pairs.append((b, to))
        return pairs

    return route


def across_z(count):
    return [(b, b ^ RING) for b in range(count)]


def permute(value, route):
    return lax.ppermute(value, AXES, route(lax.axis_size(AXES)))


def softmax_parts(logits):
    powers = jnp.exp2(logits - jnp.max(logits, axis=0, keepdims=True))
    return powers, jnp.sum(powers, axis=0, keepdims=True)


def from_slots(place, sources, act):
    if len(sources) == SPAN:
        for distance in range(SPAN):
            act(distance, sources[distance])
        return
    own, onward, own2, rotated, landed, back = sources
    act(0, own)
    act(1, onward)
    for distance, here, earlier in ((2, own2, back), (3, rotated, landed)):
        pl.when(place >= distance)(functools.partial(act, distance, here))
        pl.when(place < distance)(functools.partial(act, distance, earlier))


def pack_kernel(latent_ref, rope_ref, key_ref, first_ref, rest_ref, turned_ref, sems):
    rope_copy = pltpu.make_async_copy(rope_ref, turned_ref, sems.at[3])
    rope_copy.start()
    copies = [
        pltpu.make_async_copy(key_ref.at[:, pl.ds(0, CUT)], first_ref.at[:, pl.ds(0, CUT)], sems.at[0]),
        pltpu.make_async_copy(latent_ref, first_ref.at[:, pl.ds(CUT, LATENT)], sems.at[1]),
        pltpu.make_async_copy(key_ref.at[:, pl.ds(CUT, REST)], rest_ref, sems.at[2]),
    ]
    for copy in copies:
        copy.start()
    rope_copy.wait()
    rope = turned_ref[...].astype(jnp.float32)
    both = jnp.concatenate([rope, rope], axis=0).T.astype(jnp.bfloat16)
    first_ref[:, CUT + LATENT :] = both
    for copy in copies:
        copy.wait()


def absorb_kernel(nope_ref, rope_ref, up_ref, mixed_ref):
    lane = lax.broadcasted_iota(jnp.int32, (TOK, 2 * ROPE), 1)
    for head in range(HEADS):
        rows = slice(head * TOK, (head + 1) * TOK)
        absorbed = dot(nope_ref[:, head * HEAD : (head + 1) * HEAD], up_ref[head])
        mixed_ref[rows, :LATENT] = absorbed.astype(jnp.bfloat16)
        rope = rope_ref[:, (head // 2) * 2 * ROPE : (head // 2 + 1) * 2 * ROPE]
        kept = (lane < ROPE) if head % 2 == 0 else (lane >= ROPE)
        mixed_ref[rows, LATENT:] = jnp.where(kept, rope, jnp.zeros_like(rope))


def student_kernel(scalar_ref, length_ref, kl_ref, mixed_ref, *refs):
    sources, (p_ref, bias_ref, coeff_ref, lrt_ref, lr_ref, sems) = refs[:SPAN], refs[SPAN:]
    position = scalar_ref[0]
    place = position % RING

    def copy(distance, source):
        return pltpu.make_async_copy(
            source.at[:, pl.ds(CUT, WIDE)],
            lr_ref.at[pl.ds(distance * TOK, TOK)],
            sems.at[distance],
        )

    from_slots(place, sources, lambda distance, source: copy(distance, source).start())
    query = lax.broadcasted_iota(jnp.int32, (TOK, TOK), 1)
    key = lax.broadcasted_iota(jnp.int32, (TOK, TOK), 0)
    for distance in range(SPAN):
        length = length_ref[jnp.maximum(position - distance, 0)]
        length = jnp.where(distance <= scalar_ref[1], length, 0)
        allowed = key < length
        if distance == 0:
            allowed = allowed & (key <= query)
        bias_ref[distance * TOK : (distance + 1) * TOK, :] = jnp.where(allowed, 0.0, -1e30)
    live = lax.broadcasted_iota(jnp.int32, (HEADS, TOK), 1) < length_ref[position]
    coeff_ref[...] = jnp.where(live, kl_ref[...], 0.0)
    for distance in range(SPAN):
        copy(distance, sources[distance]).wait()
    for pair in range(PAIRS):
        logits = dot(lr_ref[...], mixed_ref[pair * 2 * TOK : (pair + 1) * 2 * TOK, :], NT)
        for half in range(2):
            head = 2 * pair + half
            powers, total = softmax_parts(
                logits[:, half * TOK : (half + 1) * TOK] * (F_STUDENT * LOG2E) + bias_ref[...]
            )
            weight = coeff_ref[head : head + 1, :]
            p_ref[:, head * TOK : (head + 1) * TOK] = powers * (weight / total)
    lrt_ref[...] = lr_ref[...].T


def teacher_kernel(first, pairs, start, scalar_ref, *refs):
    count = len(start)
    last = first > 0
    sources, refs = refs[:count], refs[count:]
    (query_ref, p_ref, bias_ref, coeff_ref, mixed_ref), refs = refs[:5], refs[5:]
    if last:
        sum_ref, g_ref, own_ref, *sent_refs = refs[:6]
    else:
        g_ref, sum_out_ref = refs[:2]
    keys_ref, diagonal_ref, sems = refs[-3:]
    place = scalar_ref[0] % RING
    columns = dict(zip(map(id, sources), start))

    def copy(pair, distance, source):
        return pltpu.make_async_copy(
            source.at[:, pl.ds(columns[id(source)] + pair * 2 * HEAD, 2 * HEAD)],
            keys_ref.at[pair, pl.ds(distance * TOK, TOK)],
            sems.at[pair, distance],
        )

    for pair in range(pairs):
        from_slots(
            place, sources, lambda distance, source, pair=pair: copy(pair, distance, source).start()
        )
    diagonal_ref[...] = jnp.zeros_like(diagonal_ref)
    for pair in range(pairs):
        for half in range(2):
            block = slice(half * HEAD, (half + 1) * HEAD)
            head = 2 * pair + half
            diagonal_ref[pair, block, block] = query_ref[:, (2 * first + head) * HEAD : (2 * first + head + 1) * HEAD]
    for pair in range(pairs):
        for distance in range(SPAN):
            copy(pair, distance, sources[distance]).wait()
    for pair in range(pairs):
        logits = dot(keys_ref[pair], diagonal_ref[pair], NT)
        for half in range(2):
            head = 2 * pair + half
            powers, total = softmax_parts(
                logits[:, half * TOK : (half + 1) * TOK] * (F_TEACHER * LOG2E) + bias_ref[...]
            )
            full = 2 * first + head
            weight = coeff_ref[full : full + 1, :]
            student = p_ref[:, full * TOK : (full + 1) * TOK]
            g_ref[:, head * TOK : (head + 1) * TOK] = (student - powers * (weight / total)).astype(jnp.bfloat16)
    summed = dot(g_ref[...], mixed_ref[2 * first * TOK : 2 * (first + pairs) * TOK, :])
    if last:
        summed = (summed + sum_ref[...]) * F_STUDENT
        own_ref[...] = summed[:TOK]
        for distance in range(1, SPAN):
            sent_refs[distance - 1][...] = summed[distance * TOK : (distance + 1) * TOK].astype(
                jnp.bfloat16
            )
    else:
        sum_out_ref[...] = summed


def query_kernel(counts, *refs):
    g_refs, (lrt_ref, up_ref, nope_out_ref, rope_out_ref) = refs[: len(counts)], refs[len(counts) :]
    head = 0
    for g_ref, pairs in zip(g_refs, counts):
        for pair in range(pairs):
            grads = dot(lrt_ref[...], g_ref[:, pair * 2 * TOK : (pair + 1) * 2 * TOK]) * F_STUDENT
            grads = grads.astype(jnp.bfloat16)
            ropes = []
            for half in range(2):
                block = slice(half * TOK, (half + 1) * TOK)
                turned = dot(up_ref[head + half], grads[:LATENT, block])
                nope_out_ref[:, (head + half) * HEAD : (head + half + 1) * HEAD] = turned.T.astype(
                    jnp.bfloat16
                )
                ropes.append(grads[LATENT + half * ROPE : LATENT + (half + 1) * ROPE, block])
            both = jnp.concatenate(ropes, axis=0).astype(jnp.float32).T.astype(jnp.bfloat16)
            rope_out_ref[:, head * ROPE : (head + 2) * ROPE] = both
            head += 2


def shape(*dims, dtype=jnp.bfloat16):
    return jax.ShapeDtypeStruct(dims, dtype)


SMEM = pl.BlockSpec(memory_space=pltpu.SMEM)
ANY = pl.BlockSpec(memory_space=pl.ANY)
VMEM = pl.BlockSpec(memory_space=pltpu.VMEM)
HBM = pl.BlockSpec(memory_space=pltpu.HBM)


def call(kernel, ins, outs, scratch, flops, accessed, exps=0, kept=True):
    return pl.pallas_call(
        kernel,
        in_specs=ins,
        out_specs=[VMEM] * len(outs),
        out_shape=[pltpu.VMEM(form.shape, form.dtype) for form in outs] if kept else outs,
        scratch_shapes=scratch,
        compiler_params=pltpu.CompilerParams(vmem_limit_bytes=VMEM_LIMIT),
        cost_estimate=pl.CostEstimate(flops=flops, bytes_accessed=accessed, transcendentals=exps),
    )


def finish_kernel(kept_ref, one_ref, two_ref, three_ref, latent_ref, rope_ref):
    total = kept_ref[...]
    for ref in (one_ref, two_ref, three_ref):
        total = total + ref[...].astype(jnp.float32)
    latent_ref[...] = total[:, :LATENT]
    turned = total[:, LATENT:].T
    rope_ref[...] = turned[:ROPE] + turned[ROPE:]


def pack_call(latent, key_rope, teacher_key):
    return call(
        pack_kernel,
        [HBM] * 3,
        [shape(TOK, CUT + WIDE), shape(TOK, REST)],
        [pltpu.VMEM((ROPE, TOK), jnp.bfloat16), pltpu.SemaphoreType.DMA((4,))],
        0,
        2_000_000,
    )(*(pltpu.with_memory_space_constraint(a, pltpu.HBM) for a in (latent, key_rope.T, teacher_key)))


def absorb_call(nope, rope, up_weight):
    return call(
        absorb_kernel,
        [VMEM] * 3,
        [shape(HEADS * TOK, WIDE)],
        [],
        2 * HEADS * TOK * HEAD * LATENT,
        6_000_000,
    )(nope, rope, up_weight)[0]


def student_call(scalars, valid_len, kl_weight, mixed, sources):
    return call(
        student_kernel,
        [SMEM, SMEM, VMEM, VMEM] + [ANY] * SPAN,
        [
            shape(KEYS, HEADS * TOK, dtype=jnp.float32),
            shape(KEYS, TOK, dtype=jnp.float32),
            shape(HEADS, TOK, dtype=jnp.float32),
            shape(WIDE, KEYS),
        ],
        [pltpu.VMEM((KEYS, WIDE), jnp.bfloat16), pltpu.SemaphoreType.DMA((SPAN,))],
        2 * HEADS * TOK * KEYS * WIDE,
        8_000_000,
        HEADS * TOK * KEYS,
    )(scalars, valid_len, kl_weight.T, mixed, *sources)


def teacher_call(first, pairs, start, scalars, sources, *operands):
    outs = [shape(KEYS, pairs * 2 * TOK)]
    if first > 0:
        outs += [shape(TOK, WIDE, dtype=jnp.float32)] + [shape(TOK, WIDE)] * 3
    else:
        outs += [shape(KEYS, WIDE, dtype=jnp.float32)]
    return call(
        functools.partial(teacher_kernel, first, pairs, start),
        [SMEM] + [ANY] * len(sources) + [VMEM] * len(operands),
        outs,
        [
            pltpu.VMEM((pairs, KEYS, 2 * HEAD), jnp.bfloat16),
            pltpu.VMEM((pairs, 2 * TOK, 2 * HEAD), jnp.bfloat16),
            pltpu.SemaphoreType.DMA((pairs, SPAN)),
        ],
        4 * pairs * TOK * KEYS * (2 * HEAD + WIDE),
        pairs * 1_500_000,
        2 * pairs * TOK * KEYS,
    )(scalars, *sources, *operands)


def query_call(counts, gs, lrt, up_weight):
    return call(
        functools.partial(query_kernel, counts),
        [VMEM] * (len(counts) + 2),
        [shape(TOK, HEADS * HEAD), shape(TOK, HEADS * ROPE)],
        [],
        4 * HEADS * TOK * LATENT * (KEYS + HEAD),
        6_000_000,
        kept=False,
    )(*gs, lrt, up_weight)


def finish_call(kept, received):
    return call(
        finish_kernel,
        [VMEM] * 4,
        [shape(TOK, LATENT, dtype=jnp.float32), shape(ROPE, TOK, dtype=jnp.float32)],
        [],
        0,
        1_000_000,
        kept=False,
    )(kept, *received)


def after(value, *others):
    return lax.optimization_barrier((value,) + others)[0]


def on_device(
    query_nope,
    query_rope,
    latent,
    key_rope,
    teacher_query,
    teacher_key,
    up_weight,
    kl_weight,
    key_back,
    valid_len,
):
    position = lax.axis_index(AXES)
    place = position % RING
    scalars = jnp.stack([position.astype(jnp.int32), key_back[0]])
    first, rest = pack_call(latent, key_rope, teacher_key)

    rotated = permute(rest, along_x(-1, (0, 1, 2, 3)))
    crossed_first = permute(first, across_z)
    leaving = jnp.where(place == RING - 1, rest, rotated)
    crossed = permute(leaving, across_z)
    later = after(rest, leaving)
    own2 = permute(later, along_x(2, (0, 1)))
    everywhere = (0, 1, 2, 3)
    spread = [
        permute(
            jnp.where(place + step >= RING, crossed_first, first),
            along_x(step, everywhere, everywhere[RING - step :]),
        )
        for step in (1, 2, 3)
    ]
    mixed = absorb_call(after(query_nope, crossed, own2), query_rope, up_weight)
    chunk = (first, *spread)
    p, bias, coeff, lrt = student_call(
        scalars, valid_len, kl_weight, mixed, chunk
    )
    back = permute(crossed, along_x(-1, (1, 2), (1, 2)))
    onward = permute(jnp.where(place == RING - 1, crossed, rest), along_x(1, everywhere, (3,)))
    landed = permute(crossed, along_x(0, (0, 1, 2), (0, 1, 2)))

    shared = (teacher_query, p, bias, coeff, mixed)
    g0, summed = teacher_call(0, FIRST, [0] * SPAN, scalars, chunk, *shared)
    chunk = (rest, onward, own2, rotated, landed, back)
    g1, kept, *sent = teacher_call(FIRST, PAIRS - FIRST, [0] * 6, scalars, chunk, *shared, summed)

    received = [
        lax.ppermute(
            sent[distance - 1],
            AXES,
            [(b, b - distance) for b in range(distance, lax.axis_size(AXES))],
        )
        for distance in range(1, SPAN)
    ]
    d_nope, d_rope = query_call((FIRST, PAIRS - FIRST), (g0, g1), lrt, up_weight)
    d_latent, d_key_rope = finish_call(kept, received)
    return d_nope, d_rope, d_latent, d_key_rope.T


def solution(mesh):
    split = P(AXES, None)
    return jax.shard_map(
        on_device,
        mesh=mesh,
        in_specs=(split,) * 6 + (P(), split, P(AXES), P()),
        out_specs=(split,) * 4,
        check_vma=False,
    )
```

```python
import functools
import math

import jax
import jax.numpy as jnp
from jax import lax
from jax.experimental import pallas as pl
from jax.experimental.pallas import tpu as pltpu
from jax.sharding import PartitionSpec as P

HEADS = 16
HEAD = 128
LATENT = 512
ROPE = 64
TOK = 128
SPAN = 4
KEYS = SPAN * TOK
WIDE = LATENT + 2 * ROPE
PAIRS = HEADS // 2
FIRST = 3
CUT = FIRST * 2 * HEAD
REST = HEADS * HEAD - CUT
RING = 4
AXES = ("outer", "inner")
F_STUDENT = 1.0 / math.sqrt(HEAD + ROPE)
F_TEACHER = 1.0 / math.sqrt(HEAD)
LOG2E = math.log2(math.e)
VMEM_LIMIT = 20 * 1024 * 1024

NN = (((1,), (0,)), ((), ()))
NT = (((1,), (1,)), ((), ()))


def dot(a, b, dims=NN):
    return lax.dot_general(a, b, dims, preferred_element_type=jnp.float32)


def along_x(step, sources, leaves=None):
    def route(count):
        pairs = []
        for b in range(count):
            if b % RING in sources:
                to = b - b % RING + (b + step) % RING
                if leaves is not None and b % RING in leaves and b % (2 * RING) < RING:
                    to += 2 * RING
                if to < count:
                    pairs.append((b, to))
        return pairs

    return route


def across_z(count):
    return [(b, b ^ RING) for b in range(count)]


def permute(value, route):
    return lax.ppermute(value, AXES, route(lax.axis_size(AXES)))


def softmax_parts(logits):
    powers = jnp.exp2(logits - jnp.max(logits, axis=0, keepdims=True))
    return powers, jnp.sum(powers, axis=0, keepdims=True)


def from_slots(place, sources, act):
    if len(sources) == SPAN:
        for distance in range(SPAN):
            act(distance, sources[distance])
        return
    own, onward, own2, rotated, landed, back = sources
    act(0, own)
    act(1, onward)
    for distance, here, earlier in ((2, own2, back), (3, rotated, landed)):
        pl.when(place >= distance)(functools.partial(act, distance, here))
        pl.when(place < distance)(functools.partial(act, distance, earlier))


def pack_kernel(latent_ref, rope_ref, key_ref, first_ref, rest_ref, turned_ref, sems):
    rope_copy = pltpu.make_async_copy(rope_ref, turned_ref, sems.at[3])
    rope_copy.start()
    copies = [
        pltpu.make_async_copy(key_ref.at[:, pl.ds(0, CUT)], first_ref.at[:, pl.ds(0, CUT)], sems.at[0]),
        pltpu.make_async_copy(latent_ref, first_ref.at[:, pl.ds(CUT, LATENT)], sems.at[1]),
        pltpu.make_async_copy(key_ref.at[:, pl.ds(CUT, REST)], rest_ref, sems.at[2]),
    ]
    for copy in copies:
        copy.start()
    rope_copy.wait()
    rope = turned_ref[...].astype(jnp.float32)
    both = jnp.concatenate([rope, rope], axis=0).T.astype(jnp.bfloat16)
    first_ref[:, CUT + LATENT :] = both
    for copy in copies:
        copy.wait()


def absorb_kernel(nope_ref, rope_ref, up_ref, mixed_ref):
    lane = lax.broadcasted_iota(jnp.int32, (TOK, 2 * ROPE), 1)
    for head in range(HEADS):
        rows = slice(head * TOK, (head + 1) * TOK)
        absorbed = dot(nope_ref[:, head * HEAD : (head + 1) * HEAD], up_ref[head])
        mixed_ref[rows, :LATENT] = absorbed.astype(jnp.bfloat16)
        rope = rope_ref[:, (head // 2) * 2 * ROPE : (head // 2 + 1) * 2 * ROPE]
        kept = (lane < ROPE) if head % 2 == 0 else (lane >= ROPE)
        mixed_ref[rows, LATENT:] = jnp.where(kept, rope, jnp.zeros_like(rope))


def student_kernel(scalar_ref, length_ref, kl_ref, mixed_ref, *refs):
    sources, (p_ref, bias_ref, coeff_ref, lrt_ref, lr_ref, sems) = refs[:SPAN], refs[SPAN:]
    position = scalar_ref[0]
    place = position % RING

    def copy(distance, source):
        return pltpu.make_async_copy(
            source.at[:, pl.ds(CUT, WIDE)],
            lr_ref.at[pl.ds(distance * TOK, TOK)],
            sems.at[distance],
        )

    from_slots(place, sources, lambda distance, source: copy(distance, source).start())
    query = lax.broadcasted_iota(jnp.int32, (TOK, TOK), 1)
    key = lax.broadcasted_iota(jnp.int32, (TOK, TOK), 0)
    for distance in range(SPAN):
        length = length_ref[jnp.maximum(position - distance, 0)]
        length = jnp.where(distance <= scalar_ref[1], length, 0)
        allowed = key < length
        if distance == 0:
            allowed = allowed & (key <= query)
        bias_ref[distance * TOK : (distance + 1) * TOK, :] = jnp.where(allowed, 0.0, -1e30)
    live = lax.broadcasted_iota(jnp.int32, (HEADS, TOK), 1) < length_ref[position]
    coeff_ref[...] = jnp.where(live, kl_ref[...], 0.0)
    for distance in range(SPAN):
        copy(distance, sources[distance]).wait()
    for pair in range(PAIRS):
        logits = dot(lr_ref[...], mixed_ref[pair * 2 * TOK : (pair + 1) * 2 * TOK, :], NT)
        for half in range(2):
            head = 2 * pair + half
            powers, total = softmax_parts(
                logits[:, half * TOK : (half + 1) * TOK] * (F_STUDENT * LOG2E) + bias_ref[...]
            )
            weight = coeff_ref[head : head + 1, :]
            p_ref[:, head * TOK : (head + 1) * TOK] = powers * (weight / total)
    lrt_ref[...] = lr_ref[...].T


def teacher_kernel(first, pairs, start, scalar_ref, *refs):
    count = len(start)
    last = first > 0
    sources, refs = refs[:count], refs[count:]
    (query_ref, p_ref, bias_ref, coeff_ref, mixed_ref), refs = refs[:5], refs[5:]
    if last:
        sum_ref, g_ref, own_ref, *sent_refs = refs[:6]
    else:
        g_ref, sum_out_ref = refs[:2]
    keys_ref, diagonal_ref, sems = refs[-3:]
    place = scalar_ref[0] % RING
    columns = dict(zip(map(id, sources), start))

    def copy(pair, distance, source):
        return pltpu.make_async_copy(
            source.at[:, pl.ds(columns[id(source)] + pair * 2 * HEAD, 2 * HEAD)],
            keys_ref.at[pair, pl.ds(distance * TOK, TOK)],
            sems.at[pair, distance],
        )

    for pair in range(pairs):
        from_slots(
            place, sources, lambda distance, source, pair=pair: copy(pair, distance, source).start()
        )
    diagonal_ref[...] = jnp.zeros_like(diagonal_ref)
    for pair in range(pairs):
        for half in range(2):
            block = slice(half * HEAD, (half + 1) * HEAD)
            head = 2 * pair + half
            diagonal_ref[pair, block, block] = query_ref[:, (2 * first + head) * HEAD : (2 * first + head + 1) * HEAD]
    for pair in range(pairs):
        for distance in range(SPAN):
            copy(pair, distance, sources[distance]).wait()
    for pair in range(pairs):
        logits = dot(keys_ref[pair], diagonal_ref[pair], NT)
        for half in range(2):
            head = 2 * pair + half
            powers, total = softmax_parts(
                logits[:, half * TOK : (half + 1) * TOK] * (F_TEACHER * LOG2E) + bias_ref[...]
            )
            full = 2 * first + head
            weight = coeff_ref[full : full + 1, :]
            student = p_ref[:, full * TOK : (full + 1) * TOK]
            g_ref[:, head * TOK : (head + 1) * TOK] = (student - powers * (weight / total)).astype(jnp.bfloat16)
    summed = dot(g_ref[...], mixed_ref[2 * first * TOK : 2 * (first + pairs) * TOK, :])
    if last:
        summed = (summed + sum_ref[...]) * F_STUDENT
        own_ref[...] = summed[:TOK]
        for distance in range(1, SPAN):
            sent_refs[distance - 1][...] = summed[distance * TOK : (distance + 1) * TOK].astype(
                jnp.bfloat16
            )
    else:
        sum_out_ref[...] = summed


def query_kernel(counts, *refs):
    g_refs, (lrt_ref, up_ref, nope_out_ref, rope_out_ref) = refs[: len(counts)], refs[len(counts) :]
    head = 0
    for g_ref, pairs in zip(g_refs, counts):
        for pair in range(pairs):
            grads = dot(lrt_ref[...], g_ref[:, pair * 2 * TOK : (pair + 1) * 2 * TOK]) * F_STUDENT
            grads = grads.astype(jnp.bfloat16)
            ropes = []
            for half in range(2):
                block = slice(half * TOK, (half + 1) * TOK)
                turned = dot(up_ref[head + half], grads[:LATENT, block])
                nope_out_ref[:, (head + half) * HEAD : (head + half + 1) * HEAD] = turned.T.astype(
                    jnp.bfloat16
                )
                ropes.append(grads[LATENT + half * ROPE : LATENT + (half + 1) * ROPE, block])
            both = jnp.concatenate(ropes, axis=0).astype(jnp.float32).T.astype(jnp.bfloat16)
            rope_out_ref[:, head * ROPE : (head + 2) * ROPE] = both
            head += 2


def shape(*dims, dtype=jnp.bfloat16):
    return jax.ShapeDtypeStruct(dims, dtype)


SMEM = pl.BlockSpec(memory_space=pltpu.SMEM)
ANY = pl.BlockSpec(memory_space=pl.ANY)
VMEM = pl.BlockSpec(memory_space=pltpu.VMEM)
HBM = pl.BlockSpec(memory_space=pltpu.HBM)


def call(kernel, ins, outs, scratch, flops, accessed, exps=0, kept=True):
    return pl.pallas_call(
        kernel,
        in_specs=ins,
        out_specs=[VMEM] * len(outs),
        out_shape=[pltpu.VMEM(form.shape, form.dtype) for form in outs] if kept else outs,
        scratch_shapes=scratch,
        compiler_params=pltpu.CompilerParams(vmem_limit_bytes=VMEM_LIMIT),
        cost_estimate=pl.CostEstimate(flops=flops, bytes_accessed=accessed, transcendentals=exps),
    )


def finish_kernel(kept_ref, one_ref, two_ref, three_ref, latent_ref, rope_ref):
    total = kept_ref[...]
    for ref in (one_ref, two_ref, three_ref):
        total = total + ref[...].astype(jnp.float32)
    latent_ref[...] = total[:, :LATENT]
    turned = total[:, LATENT:].T
    rope_ref[...] = turned[:ROPE] + turned[ROPE:]


def pack_call(latent, key_rope, teacher_key):
    return call(
        pack_kernel,
        [HBM] * 3,
        [shape(TOK, CUT + WIDE), shape(TOK, REST)],
        [pltpu.VMEM((ROPE, TOK), jnp.bfloat16), pltpu.SemaphoreType.DMA((4,))],
        0,
        2_000_000,
    )(*(pltpu.with_memory_space_constraint(a, pltpu.HBM) for a in (latent, key_rope.T, teacher_key)))


def absorb_call(nope, rope, up_weight):
    return call(
        absorb_kernel,
        [VMEM] * 3,
        [shape(HEADS * TOK, WIDE)],
        [],
        2 * HEADS * TOK * HEAD * LATENT,
        6_000_000,
    )(nope, rope, up_weight)[0]


def student_call(scalars, valid_len, kl_weight, mixed, sources):
    return call(
        student_kernel,
        [SMEM, SMEM, VMEM, VMEM] + [ANY] * SPAN,
        [
            shape(KEYS, HEADS * TOK, dtype=jnp.float32),
            shape(KEYS, TOK, dtype=jnp.float32),
            shape(HEADS, TOK, dtype=jnp.float32),
            shape(WIDE, KEYS),
        ],
        [pltpu.VMEM((KEYS, WIDE), jnp.bfloat16), pltpu.SemaphoreType.DMA((SPAN,))],
        2 * HEADS * TOK * KEYS * WIDE,
        8_000_000,
        HEADS * TOK * KEYS,
    )(scalars, valid_len, kl_weight.T, mixed, *sources)


def teacher_call(first, pairs, start, scalars, sources, *operands):
    outs = [shape(KEYS, pairs * 2 * TOK)]
    if first > 0:
        outs += [shape(TOK, WIDE, dtype=jnp.float32)] + [shape(TOK, WIDE)] * 3
    else:
        outs += [shape(KEYS, WIDE, dtype=jnp.float32)]
    return call(
        functools.partial(teacher_kernel, first, pairs, start),
        [SMEM] + [ANY] * len(sources) + [VMEM] * len(operands),
        outs,
        [
            pltpu.VMEM((pairs, KEYS, 2 * HEAD), jnp.bfloat16),
            pltpu.VMEM((pairs, 2 * TOK, 2 * HEAD), jnp.bfloat16),
            pltpu.SemaphoreType.DMA((pairs, SPAN)),
        ],
        4 * pairs * TOK * KEYS * (2 * HEAD + WIDE),
        pairs * 1_500_000,
        2 * pairs * TOK * KEYS,
    )(scalars, *sources, *operands)


def query_call(counts, gs, lrt, up_weight):
    return call(
        functools.partial(query_kernel, counts),
        [VMEM] * (len(counts) + 2),
        [shape(TOK, HEADS * HEAD), shape(TOK, HEADS * ROPE)],
        [],
        4 * HEADS * TOK * LATENT * (KEYS + HEAD),
        6_000_000,
        kept=False,
    )(*gs, lrt, up_weight)


def finish_call(kept, received):
    return call(
        finish_kernel,
        [VMEM] * 4,
        [shape(TOK, LATENT, dtype=jnp.float32), shape(ROPE, TOK, dtype=jnp.float32)],
        [],
        0,
        1_000_000,
        kept=False,
    )(kept, *received)


def after(value, *others):
    return lax.optimization_barrier((value,) + others)[0]


def on_device(
    query_nope,
    query_rope,
    latent,
    key_rope,
    teacher_query,
    teacher_key,
    up_weight,
    kl_weight,
    key_back,
    valid_len,
):
    position = lax.axis_index(AXES)
    place = position % RING
    scalars = jnp.stack([position.astype(jnp.int32), key_back[0]])
    first, rest = pack_call(latent, key_rope, teacher_key)

    rotated = permute(rest, along_x(-1, (0, 1, 2, 3)))
    crossed_first = permute(first, across_z)
    leaving = jnp.where(place == RING - 1, rest, rotated)
    crossed = permute(leaving, across_z)
    later = after(rest, leaving)
    own2 = permute(later, along_x(2, (0, 1)))
    everywhere = (0, 1, 2, 3)
    spread = [
        permute(
            jnp.where(place + step >= RING, crossed_first, first),
            along_x(step, everywhere, everywhere[RING - step :]),
        )
        for step in (1, 2, 3)
    ]
    mixed = absorb_call(after(query_nope, crossed, own2), query_rope, up_weight)
    chunk = (first, *spread)
    p, bias, coeff, lrt = student_call(
        scalars, valid_len, kl_weight, mixed, chunk
    )
    back = permute(crossed, along_x(-1, (1, 2), (1, 2)))
    onward = permute(jnp.where(place == RING - 1, crossed, rest), along_x(1, everywhere, (3,)))
    landed = permute(crossed, along_x(0, (0, 1, 2), (0, 1, 2)))

    shared = (teacher_query, p, bias, coeff, mixed)
    g0, summed = teacher_call(0, FIRST, [0] * SPAN, scalars, chunk, *shared)
    chunk = (rest, onward, own2, rotated, landed, back)
    g1, kept, *sent = teacher_call(FIRST, PAIRS - FIRST, [0] * 6, scalars, chunk, *shared, summed)

    received = [
        lax.ppermute(
            sent[distance - 1],
            AXES,
            [(b, b - distance) for b in range(distance, lax.axis_size(AXES))],
        )
        for distance in (3, 1, 2)
    ]
    d_nope, d_rope = query_call((FIRST, PAIRS - FIRST), (g0, g1), lrt, up_weight)
    d_latent, d_key_rope = finish_call(kept, received)
    return d_nope, d_rope, d_latent, d_key_rope.T


def solution(mesh):
    split = P(AXES, None)
    return jax.shard_map(
        on_device,
        mesh=mesh,
        in_specs=(split,) * 6 + (P(), split, P(AXES), P()),
        out_specs=(split,) * 4,
        check_vma=False,
    )
```

```python
import functools
import math

import jax
import jax.numpy as jnp
from jax import lax
from jax.experimental import pallas as pl
from jax.experimental.pallas import tpu as pltpu
from jax.sharding import PartitionSpec as P

HEADS = 16
HEAD = 128
LATENT = 512
ROPE = 64
TOK = 128
SPAN = 4
KEYS = SPAN * TOK
WIDE = LATENT + 2 * ROPE
PAIRS = HEADS // 2
FIRST = 3
CUT = FIRST * 2 * HEAD
REST = HEADS * HEAD - CUT
RING = 4
AXES = ("outer", "inner")
F_STUDENT = 1.0 / math.sqrt(HEAD + ROPE)
F_TEACHER = 1.0 / math.sqrt(HEAD)
LOG2E = math.log2(math.e)
VMEM_LIMIT = 20 * 1024 * 1024

NN = (((1,), (0,)), ((), ()))
NT = (((1,), (1,)), ((), ()))


def dot(a, b, dims=NN):
    return lax.dot_general(a, b, dims, preferred_element_type=jnp.float32)


def along_x(step, sources, leaves=None):
    def route(count):
        pairs = []
        for b in range(count):
            if b % RING in sources:
                to = b - b % RING + (b + step) % RING
                if leaves is not None and b % RING in leaves and b % (2 * RING) < RING:
                    to += 2 * RING
                if to < count:
                    pairs.append((b, to))
        return pairs

    return route


def across_z(count):
    return [(b, b ^ RING) for b in range(count)]


def permute(value, route):
    return lax.ppermute(value, AXES, route(lax.axis_size(AXES)))


def softmax_parts(logits):
    powers = jnp.exp2(logits - jnp.max(logits, axis=0, keepdims=True))
    return powers, jnp.sum(powers, axis=0, keepdims=True)


def from_slots(place, sources, act):
    if len(sources) == SPAN:
        for distance in range(SPAN):
            act(distance, sources[distance])
        return
    own, onward, own2, rotated, landed, back = sources
    act(0, own)
    act(1, onward)
    for distance, here, earlier in ((2, own2, back), (3, rotated, landed)):
        pl.when(place >= distance)(functools.partial(act, distance, here))
        pl.when(place < distance)(functools.partial(act, distance, earlier))


def pack_kernel(latent_ref, rope_ref, key_ref, first_ref, rest_ref, turned_ref, sems):
    rope_copy = pltpu.make_async_copy(rope_ref, turned_ref, sems.at[3])
    rope_copy.start()
    copies = [
        pltpu.make_async_copy(key_ref.at[:, pl.ds(0, CUT)], first_ref.at[:, pl.ds(0, CUT)], sems.at[0]),
        pltpu.make_async_copy(latent_ref, first_ref.at[:, pl.ds(CUT, LATENT)], sems.at[1]),
        pltpu.make_async_copy(key_ref.at[:, pl.ds(CUT, REST)], rest_ref, sems.at[2]),
    ]
    for copy in copies:
        copy.start()
    rope_copy.wait()
    rope = turned_ref[...].astype(jnp.float32)
    both = jnp.concatenate([rope, rope], axis=0).T.astype(jnp.bfloat16)
    first_ref[:, CUT + LATENT :] = both
    for copy in copies:
        copy.wait()


def absorb_kernel(nope_ref, rope_ref, up_ref, mixed_ref):
    lane = lax.broadcasted_iota(jnp.int32, (TOK, 2 * ROPE), 1)
    for head in range(HEADS):
        rows = slice(head * TOK, (head + 1) * TOK)
        absorbed = dot(nope_ref[:, head * HEAD : (head + 1) * HEAD], up_ref[head])
        mixed_ref[rows, :LATENT] = absorbed.astype(jnp.bfloat16)
        rope = rope_ref[:, (head // 2) * 2 * ROPE : (head // 2 + 1) * 2 * ROPE]
        kept = (lane < ROPE) if head % 2 == 0 else (lane >= ROPE)
        mixed_ref[rows, LATENT:] = jnp.where(kept, rope, jnp.zeros_like(rope))


def student_kernel(scalar_ref, length_ref, kl_ref, mixed_ref, *refs):
    sources, (p_ref, bias_ref, coeff_ref, lrt_ref, lr_ref, sems) = refs[:SPAN], refs[SPAN:]
    position = scalar_ref[0]
    place = position % RING

    def copy(distance, source):
        return pltpu.make_async_copy(
            source.at[:, pl.ds(CUT, WIDE)],
            lr_ref.at[pl.ds(distance * TOK, TOK)],
            sems.at[distance],
        )

    from_slots(place, sources, lambda distance, source: copy(distance, source).start())
    query = lax.broadcasted_iota(jnp.int32, (TOK, TOK), 1)
    key = lax.broadcasted_iota(jnp.int32, (TOK, TOK), 0)
    for distance in range(SPAN):
        length = length_ref[jnp.maximum(position - distance, 0)]
        length = jnp.where(distance <= scalar_ref[1], length, 0)
        allowed = key < length
        if distance == 0:
            allowed = allowed & (key <= query)
        bias_ref[distance * TOK : (distance + 1) * TOK, :] = jnp.where(allowed, 0.0, -1e30)
    live = lax.broadcasted_iota(jnp.int32, (HEADS, TOK), 1) < length_ref[position]
    coeff_ref[...] = jnp.where(live, kl_ref[...], 0.0)
    for distance in range(SPAN):
        copy(distance, sources[distance]).wait()
    for pair in range(PAIRS):
        logits = dot(lr_ref[...], mixed_ref[pair * 2 * TOK : (pair + 1) * 2 * TOK, :], NT)
        for half in range(2):
            head = 2 * pair + half
            powers, total = softmax_parts(
                logits[:, half * TOK : (half + 1) * TOK] * (F_STUDENT * LOG2E) + bias_ref[...]
            )
            weight = coeff_ref[head : head + 1, :]
            p_ref[:, head * TOK : (head + 1) * TOK] = powers * (weight / total)
    lrt_ref[...] = lr_ref[...].T


def teacher_kernel(first, pairs, start, scalar_ref, *refs):
    count = len(start)
    last = first > 0
    sources, refs = refs[:count], refs[count:]
    (query_ref, p_ref, bias_ref, coeff_ref, mixed_ref), refs = refs[:5], refs[5:]
    if last:
        sum_ref, g_ref, own_ref, *sent_refs = refs[:6]
    else:
        g_ref, sum_out_ref = refs[:2]
    keys_ref, diagonal_ref, sems = refs[-3:]
    place = scalar_ref[0] % RING
    columns = dict(zip(map(id, sources), start))

    def copy(pair, distance, source):
        return pltpu.make_async_copy(
            source.at[:, pl.ds(columns[id(source)] + pair * 2 * HEAD, 2 * HEAD)],
            keys_ref.at[pair, pl.ds(distance * TOK, TOK)],
            sems.at[pair, distance],
        )

    for pair in range(pairs):
        from_slots(
            place, sources, lambda distance, source, pair=pair: copy(pair, distance, source).start()
        )
    diagonal_ref[...] = jnp.zeros_like(diagonal_ref)
    for pair in range(pairs):
        for half in range(2):
            block = slice(half * HEAD, (half + 1) * HEAD)
            head = 2 * pair + half
            diagonal_ref[pair, block, block] = query_ref[:, (2 * first + head) * HEAD : (2 * first + head + 1) * HEAD]
    for pair in range(pairs):
        for distance in range(SPAN):
            copy(pair, distance, sources[distance]).wait()
    for pair in range(pairs):
        logits = dot(keys_ref[pair], diagonal_ref[pair], NT)
        for half in range(2):
            head = 2 * pair + half
            powers, total = softmax_parts(
                logits[:, half * TOK : (half + 1) * TOK] * (F_TEACHER * LOG2E) + bias_ref[...]
            )
            full = 2 * first + head
            weight = coeff_ref[full : full + 1, :]
            student = p_ref[:, full * TOK : (full + 1) * TOK]
            g_ref[:, head * TOK : (head + 1) * TOK] = (student - powers * (weight / total)).astype(jnp.bfloat16)
    summed = dot(g_ref[...], mixed_ref[2 * first * TOK : 2 * (first + pairs) * TOK, :])
    if last:
        summed = (summed + sum_ref[...]) * F_STUDENT
        own_ref[...] = summed[:TOK]
        for distance in range(1, SPAN):
            sent_refs[distance - 1][...] = summed[distance * TOK : (distance + 1) * TOK].astype(
                jnp.bfloat16
            )
    else:
        sum_out_ref[...] = summed


def query_kernel(counts, *refs):
    g_refs, (lrt_ref, up_ref, nope_out_ref, rope_out_ref) = refs[: len(counts)], refs[len(counts) :]
    head = 0
    for g_ref, pairs in zip(g_refs, counts):
        for pair in range(pairs):
            grads = dot(lrt_ref[...], g_ref[:, pair * 2 * TOK : (pair + 1) * 2 * TOK]) * F_STUDENT
            grads = grads.astype(jnp.bfloat16)
            ropes = []
            for half in range(2):
                block = slice(half * TOK, (half + 1) * TOK)
                turned = dot(up_ref[head + half], grads[:LATENT, block])
                nope_out_ref[:, (head + half) * HEAD : (head + half + 1) * HEAD] = turned.T.astype(
                    jnp.bfloat16
                )
                ropes.append(grads[LATENT + half * ROPE : LATENT + (half + 1) * ROPE, block])
            both = jnp.concatenate(ropes, axis=0).astype(jnp.float32).T.astype(jnp.bfloat16)
            rope_out_ref[:, head * ROPE : (head + 2) * ROPE] = both
            head += 2


def shape(*dims, dtype=jnp.bfloat16):
    return jax.ShapeDtypeStruct(dims, dtype)


SMEM = pl.BlockSpec(memory_space=pltpu.SMEM)
ANY = pl.BlockSpec(memory_space=pl.ANY)
VMEM = pl.BlockSpec(memory_space=pltpu.VMEM)
HBM = pl.BlockSpec(memory_space=pltpu.HBM)


def call(kernel, ins, outs, scratch, flops, accessed, exps=0, kept=True):
    return pl.pallas_call(
        kernel,
        in_specs=ins,
        out_specs=[VMEM] * len(outs),
        out_shape=[pltpu.VMEM(form.shape, form.dtype) for form in outs] if kept else outs,
        scratch_shapes=scratch,
        compiler_params=pltpu.CompilerParams(vmem_limit_bytes=VMEM_LIMIT),
        cost_estimate=pl.CostEstimate(flops=flops, bytes_accessed=accessed, transcendentals=exps),
    )


def finish_kernel(kept_ref, one_ref, two_ref, three_ref, latent_ref, rope_ref):
    total = kept_ref[...]
    for ref in (one_ref, two_ref, three_ref):
        total = total + ref[...].astype(jnp.float32)
    latent_ref[...] = total[:, :LATENT]
    turned = total[:, LATENT:].T
    rope_ref[...] = turned[:ROPE] + turned[ROPE:]


def pack_call(latent, key_rope, teacher_key):
    return call(
        pack_kernel,
        [HBM] * 3,
        [shape(TOK, CUT + WIDE), shape(TOK, REST)],
        [pltpu.VMEM((ROPE, TOK), jnp.bfloat16), pltpu.SemaphoreType.DMA((4,))],
        0,
        2_000_000,
    )(*(pltpu.with_memory_space_constraint(a, pltpu.HBM) for a in (latent, key_rope.T, teacher_key)))


def absorb_call(nope, rope, up_weight):
    return call(
        absorb_kernel,
        [VMEM] * 3,
        [shape(HEADS * TOK, WIDE)],
        [],
        2 * HEADS * TOK * HEAD * LATENT,
        6_000_000,
    )(nope, rope, up_weight)[0]


def student_call(scalars, valid_len, kl_weight, mixed, sources):
    return call(
        student_kernel,
        [SMEM, SMEM, VMEM, VMEM] + [ANY] * SPAN,
        [
            shape(KEYS, HEADS * TOK, dtype=jnp.float32),
            shape(KEYS, TOK, dtype=jnp.float32),
            shape(HEADS, TOK, dtype=jnp.float32),
            shape(WIDE, KEYS),
        ],
        [pltpu.VMEM((KEYS, WIDE), jnp.bfloat16), pltpu.SemaphoreType.DMA((SPAN,))],
        2 * HEADS * TOK * KEYS * WIDE,
        8_000_000,
        HEADS * TOK * KEYS,
    )(scalars, valid_len, kl_weight.T, mixed, *sources)


def teacher_call(first, pairs, start, scalars, sources, *operands):
    outs = [shape(KEYS, pairs * 2 * TOK)]
    if first > 0:
        outs += [shape(TOK, WIDE, dtype=jnp.float32)] + [shape(TOK, WIDE)] * 3
    else:
        outs += [shape(KEYS, WIDE, dtype=jnp.float32)]
    return call(
        functools.partial(teacher_kernel, first, pairs, start),
        [SMEM] + [ANY] * len(sources) + [VMEM] * len(operands),
        outs,
        [
            pltpu.VMEM((pairs, KEYS, 2 * HEAD), jnp.bfloat16),
            pltpu.VMEM((pairs, 2 * TOK, 2 * HEAD), jnp.bfloat16),
            pltpu.SemaphoreType.DMA((pairs, SPAN)),
        ],
        4 * pairs * TOK * KEYS * (2 * HEAD + WIDE),
        pairs * 1_500_000,
        2 * pairs * TOK * KEYS,
    )(scalars, *sources, *operands)


def query_call(counts, gs, lrt, up_weight):
    return call(
        functools.partial(query_kernel, counts),
        [VMEM] * (len(counts) + 2),
        [shape(TOK, HEADS * HEAD), shape(TOK, HEADS * ROPE)],
        [],
        4 * HEADS * TOK * LATENT * (KEYS + HEAD),
        6_000_000,
        kept=False,
    )(*gs, lrt, up_weight)


def finish_call(kept, received):
    return call(
        finish_kernel,
        [VMEM] * 4,
        [shape(TOK, LATENT, dtype=jnp.float32), shape(ROPE, TOK, dtype=jnp.float32)],
        [],
        0,
        1_000_000,
        kept=False,
    )(kept, *received)


def after(value, *others):
    return lax.optimization_barrier((value,) + others)[0]


def on_device(
    query_nope,
    query_rope,
    latent,
    key_rope,
    teacher_query,
    teacher_key,
    up_weight,
    kl_weight,
    key_back,
    valid_len,
):
    position = lax.axis_index(AXES)
    place = position % RING
    scalars = jnp.stack([position.astype(jnp.int32), key_back[0]])
    first, rest = pack_call(latent, key_rope, teacher_key)

    rotated = permute(rest, along_x(-1, (0, 1, 2, 3)))
    crossed_first = permute(first, across_z)
    leaving = jnp.where(place == RING - 1, rest, rotated)
    crossed = permute(leaving, across_z)
    later = after(rest, leaving)
    own2 = permute(later, along_x(2, (0, 1)))
    everywhere = (0, 1, 2, 3)
    spread = [
        permute(
            jnp.where(place + step >= RING, crossed_first, first),
            along_x(step, everywhere, everywhere[RING - step :]),
        )
        for step in (1, 2, 3)
    ]
    mixed = absorb_call(after(query_nope, crossed, own2), query_rope, up_weight)
    chunk = (first, *spread)
    p, bias, coeff, lrt = student_call(
        scalars, valid_len, kl_weight, mixed, chunk
    )
    back = permute(crossed, along_x(-1, (1, 2), (1, 2)))
    onward = permute(jnp.where(place == RING - 1, crossed, rest), along_x(1, everywhere, (3,)))
    landed = permute(crossed, along_x(0, (0, 1, 2), (0, 1, 2)))

    shared = (teacher_query, p, bias, coeff, mixed)
    g0, summed = teacher_call(0, FIRST, [0] * SPAN, scalars, chunk, *shared)
    chunk = (rest, onward, own2, rotated, landed, back)
    g1, kept, *sent = teacher_call(FIRST, PAIRS - FIRST, [0] * 6, scalars, chunk, *shared, summed)

    received = [
        lax.ppermute(
            sent[distance - 1],
            AXES,
            [(b, b - distance) for b in range(distance, lax.axis_size(AXES))],
        )
        for distance in (2, 3, 1)
    ]
    d_nope, d_rope = query_call((FIRST, PAIRS - FIRST), (g0, g1), lrt, up_weight)
    d_latent, d_key_rope = finish_call(kept, received)
    return d_nope, d_rope, d_latent, d_key_rope.T


def solution(mesh):
    split = P(AXES, None)
    return jax.shard_map(
        on_device,
        mesh=mesh,
        in_specs=(split,) * 6 + (P(), split, P(AXES), P()),
        out_specs=(split,) * 4,
        check_vma=False,
    )
```
